256 devices in a mesh: blk: 64 (over x, y_hi, z), dp: 4 (over y_lo, core).
Axes of the slice: x: 4, y: 4 (y_hi: 2, y_lo: 2; y = y_hi * 2 + y_lo), z: 8, core: 2. Of those that a mesh axis runs over, the one named last changes fastest.
Arguments:
- tokens: bfloat16 [98304, 5120], P(('blk', 'dp')), may hold values from -6 to 6
- cotangent: bfloat16 [98304, 5120], P(('blk', 'dp')), may hold values from -0.44921875 to 0.44921875
- gate_weight: bfloat16 [8192, 5120], P('blk'), may hold values from -0.078125 to 0.078125
- up_weight: bfloat16 [8192, 5120], P('blk'), may hold values from -0.078125 to 0.078125
- down_weight: bfloat16 [8192, 5120], P('blk'), may hold values from -0.0625 to 0.0625
Outputs:
- gate_grad: bfloat16 [8192, 5120], P(('blk', 'dp'))
- up_grad: bfloat16 [8192, 5120], P(('blk', 'dp'))
- down_grad: bfloat16 [8192, 5120], P(('blk', 'dp'))
The draws below stay inside these ranges and needn't reach their ends.
All inputs are finite; a program needn't handle non-finite values.
Results may differ from the reference program's by a relative error of at most 0.005.
Values may be sent and summed in bfloat16 or wider, within the bound.
A program may use at most 128 MiB of HBM per device.

```python
import jax
import jax.numpy as jnp
from jax import lax

D = 5120
HB = 128
TOK_DEV = 384
HIDDEN_UNITS = 8192
TOKENS = 98304
N_BLK = 64
N_DP = 4


def levels(own_key, dims, shards, smallest, high):
    def one(dim, blocks):
        steps = jax.random.uniform(jax.random.fold_in(jax.random.fold_in(own_key, 6), dim), (blocks,), jnp.float32, smallest / len(shards), high / len(shards))
        return jnp.repeat(jnp.exp(steps), dims[dim] // blocks).reshape((-1,) + (1,) * (len(dims) - dim - 1))

    loudness = one(*shards[0])
    for cut in shards[1:]:
        loudness = loudness * one(*cut)
    return loudness


def noise(rng, dims, deviation, reach, pieces=(), held_as=jnp.bfloat16):
    values = deviation * jax.random.normal(rng, dims, jnp.float32)
    if pieces:
        values = values * levels(rng, dims, pieces, -0.22, 0.18)
    return jnp.clip(values, -reach, reach).astype(held_as)


def setup_inputs(seed: int = 0) -> dict:
    streams_of = jax.random.split(jax.random.key(seed), 6)
    tokens = noise(streams_of[0], (TOKENS, D), 1.0, 6.0, ((0, 256),))
    cotangent = noise(streams_of[1], (TOKENS, D), 0.07, 0.44921875, ((0, 256),))
    gate_weight = noise(streams_of[2], (HIDDEN_UNITS, D), D ** -0.5, 0.078125, ((0, 64),))
    up_weight = noise(streams_of[3], (HIDDEN_UNITS, D), D ** -0.5, 0.078125, ((0, 64),))
    down_weight = noise(streams_of[4], (HIDDEN_UNITS, D), HIDDEN_UNITS ** -0.5, 0.0625, ((0, 64),))
    return dict(tokens=tokens, cotangent=cotangent, gate_weight=gate_weight, up_weight=up_weight, down_weight=down_weight)


def block_terms(group_tokens, group_cotangent, w_gate, w_up, w_down):
    gate_pre = jnp.dot(group_tokens, w_gate.T, preferred_element_type=jnp.float32)
    up_pre = jnp.dot(group_tokens, w_up.T, preferred_element_type=jnp.float32)
    squash = jax.nn.sigmoid(gate_pre)
    hidden = (gate_pre * squash * up_pre).astype(jnp.bfloat16)
    down_term = jnp.dot(hidden.T, group_cotangent, preferred_element_type=jnp.float32)
    grad_hidden = jnp.dot(group_cotangent, w_down.T, preferred_element_type=jnp.float32)
    grad_gate_pre = (grad_hidden * up_pre * squash * (1.0 + gate_pre * (1.0 - squash))).astype(jnp.bfloat16)
    grad_up_pre = (grad_hidden * gate_pre * squash).astype(jnp.bfloat16)
    gate_term = jnp.dot(grad_gate_pre.T, group_tokens, preferred_element_type=jnp.float32)
    up_term = jnp.dot(grad_up_pre.T, group_tokens, preferred_element_type=jnp.float32)
    return gate_term, up_term, down_term


def reference(tokens, cotangent, gate_weight, up_weight, down_weight):
    token_groups = tokens.reshape(N_BLK, N_DP, TOK_DEV, D)
    cotangent_groups = cotangent.reshape(N_BLK, N_DP, TOK_DEV, D)

    def one_block(block_index):
        start = (block_index * HB).astype(jnp.int32)
        w_gate = lax.dynamic_slice_in_dim(gate_weight, start, HB, 0)
        w_up = lax.dynamic_slice_in_dim(up_weight, start, HB, 0)
        w_down = lax.dynamic_slice_in_dim(down_weight, start, HB, 0)
        sum_gate = jnp.zeros((HB, D), jnp.float32)
        sum_up = jnp.zeros((HB, D), jnp.float32)
        sum_down = jnp.zeros((HB, D), jnp.float32)
        for offset in range(2):
            section = ((block_index + offset) % N_BLK).astype(jnp.int32)
            for member in range(N_DP):
                group_tokens = token_groups[section, member]
                group_cotangent = cotangent_groups[section, member]
                gate_term, up_term, down_term = block_terms(group_tokens, group_cotangent, w_gate, w_up, w_down)
                sum_gate = sum_gate + gate_term
                sum_up = sum_up + up_term
                sum_down = sum_down + down_term
        return (sum_gate.astype(jnp.bfloat16), sum_up.astype(jnp.bfloat16), sum_down.astype(jnp.bfloat16))

    gate_all, up_all, down_all = lax.map(one_block, jnp.arange(N_BLK, dtype=jnp.int32))
    return (gate_all.reshape(HIDDEN_UNITS, D), up_all.reshape(HIDDEN_UNITS, D), down_all.reshape(HIDDEN_UNITS, D))
```

```python
import functools

import jax
import jax.numpy as jnp
from jax import lax
from jax.experimental import pallas as pl
from jax.experimental.pallas import tpu as pltpu
from jax.sharding import PartitionSpec as P

MESH = pl.DeviceIdType.MESH
NT = (((1,), (1,)), ((), ()))
NN = (((1,), (0,)), ((), ()))
Z_LEN = 8
CHUNKS = 4
SUB = 16
RELAY = (0, 1)
DIRECT = (2, 3)
BACK_FIRST = (0, 1)
ACROSS_FIRST = (2, 3)


def dot(a, b, dims):
    return lax.dot_general(a, b, dims, preferred_element_type=jnp.float32)


def f32(v):
    return v.astype(jnp.float32)


def bf16(v):
    return v.astype(jnp.bfloat16)


def kernel(
    n_blk, x_hbm, c_hbm, wg_hbm, wu_hbm, wd_hbm, out_hbm,
    xv, cv, w_own, w_in,
    own_pair_out, own_pair_in, own_sum,
    in_pair_out, in_pair_in, in_sum,
    back_out, back_in, across_in_out, across_in_in, across_out, across_own_in, final,
    load_sem, up_send, up_recv, fwd_send, fwd_recv, relay_send, relay_recv, fwd2_send, fwd2_recv,
    own_pair_send, own_pair_recv, in_pair_send, in_pair_recv,
    back_send, back_recv, across_in_send, across_in_recv, across_send, across_recv, fin_send, fin_recv,
):
    j = lax.axis_index("blk")
    r = lax.axis_index("dp")
    chip = lax.div(r, 2)
    core = lax.rem(r, 2)
    place = lax.rem(j, Z_LEN)
    flip_up = jnp.where(place == Z_LEN - 1, 1, 0)
    flip_down = jnp.where(place == 0, 1, 0)
    up_chip = lax.rem(chip + flip_up, 2)
    down_chip = lax.rem(chip + flip_down, 2)
    up = (lax.rem(j + 1, n_blk), up_chip * 2 + core)
    down = (lax.rem(j + n_blk - 1, n_blk), down_chip * 2 + core)
    across = (j, (1 - chip) * 2 + core)
    sibling = (j, chip * 2 + 1 - core)
    half = xv.shape[1] // 2
    mine = pl.ds(pl.multiple_of(core * half, half), half)
    theirs = pl.ds(pl.multiple_of((1 - core) * half, half), half)
    w_hbm = (wg_hbm, wu_hbm, wd_hbm)

    def remote(src, dst, send, recv, device):
        return pltpu.make_async_remote_copy(
            src_ref=src, dst_ref=dst, send_sem=send, recv_sem=recv, device_id=device, device_id_type=MESH
        )

    loads = []
    for m in range(3):
        for p in range(2):
            loads.append(pltpu.make_async_copy(w_hbm[m].at[p], w_own.at[:, p, m], load_sem.at[m * 2 + p]))
    load_x = pltpu.make_async_copy(x_hbm, xv, load_sem.at[6])
    load_c = pltpu.make_async_copy(c_hbm, cv, load_sem.at[7])
    for load in loads[:4]:
        load.start()
    load_x.start()
    for load in loads[4:]:
        load.start()
    load_c.start()

    barrier = pltpu.get_barrier_semaphore()
    for device in (up, down, across, sibling):
        pl.semaphore_signal(barrier, inc=1, device_id=device, device_id_type=MESH)
    pl.semaphore_wait(barrier, 4)

    pending = []

    def go(copy):
        copy.start()
        pending.append(copy)
        return copy

    up_copies = {}
    for k in RELAY + DIRECT:
        for m in range(3):
            if k in RELAY:
                src, dst = w_hbm[m].at[up_chip, k, :, mine], w_in.at[k, up_chip, m, :, mine]
            else:
                src, dst = w_hbm[m].at[:, k, :, mine], w_in.at[k, :, m, :, mine]
            up_copies[k, m] = go(remote(src, dst, up_send.at[k, m], up_recv.at[k, m], up))

    fwd, relay, fwd2 = {}, {}, {}

    def forward(k):
        for m in range(3):
            up_copies[k, m].wait_recv()
            if k in RELAY:
                piece = w_in.at[k, chip, m, :, mine]
                relay[k, m] = go(remote(piece, piece, relay_send.at[k, m], relay_recv.at[k, m], across))
            else:
                piece = w_in.at[k, :, m, :, mine]
            fwd[k, m] = go(remote(piece, piece, fwd_send.at[k, m], fwd_recv.at[k, m], sibling))

    def forward_relayed(k):
        for m in range(3):
            relay[k, m].wait_recv()
            piece = w_in.at[k, 1 - chip, m, :, mine]
            fwd2[k, m] = go(remote(piece, piece, fwd2_send.at[k, m], fwd2_recv.at[k, m], sibling))

    def arrived(k, m):
        fwd[k, m].wait_recv()
        if k in RELAY:
            fwd2[k, m].wait_recv()

    def project(w, lo, n, rows, act):
        total = None
        for s in (pl.ds(0, half), pl.ds(half, half)):
            part = w[:, :, lo:lo + n, :, s] if len(w.shape) == 5 else w[:, lo:lo + n, :, s]
            term = dot(part.reshape(rows, half), act[:, s], NT)
            total = term if total is None else total + term
        return total

    def hidden_grads(pre, grad_hidden, groups):
        tok = pre.shape[-1]
        pre = pre.reshape(groups, 2, SUB, tok)
        gate, up_pre = pre[:, 0], pre[:, 1]
        grad_hidden = grad_hidden.reshape(groups, SUB, tok)
        squash = jax.nn.sigmoid(gate)
        silu = gate * squash
        hidden = bf16(silu * up_pre)
        gg = bf16(grad_hidden * up_pre * squash * (1.0 + gate * (1.0 - squash)))
        gu = bf16(grad_hidden * silu)
        both = jnp.stack([gg, gu], axis=1).reshape(groups * 2 * SUB, tok)
        return both, hidden.reshape(groups * SUB, tok)

    own_groups = CHUNKS * 2
    for load in loads[:4]:
        load.wait()
    load_x.wait()
    pre = project(w_own, 0, 2, own_groups * 2 * SUB, xv)
    for load in loads[4:]:
        load.wait()
    load_c.wait()
    forward(0)
    grad_hidden = project(w_own, 2, 1, own_groups * SUB, cv)
    both, hidden = hidden_grads(pre, grad_hidden, own_groups)
    term = dot(both, xv[:, theirs], NN)
    own_pair_out[:, :, 0:2] = bf16(term).reshape(CHUNKS, 2, 2, SUB, half)
    term = dot(hidden, cv[:, theirs], NN)
    own_pair_out[:, :, 2:3] = bf16(term).reshape(CHUNKS, 2, 1, SUB, half)
    own_pair = go(remote(own_pair_out, own_pair_in, own_pair_send, own_pair_recv, sibling))
    term = dot(both, xv[:, mine], NN)
    own_sum[:, :, 0:2] = term.reshape(CHUNKS, 2, 2, SUB, half)
    term = dot(hidden, cv[:, mine], NN)
    own_sum[:, :, 2:3] = term.reshape(CHUNKS, 2, 1, SUB, half)
    forward_relayed(0)
    forward(1)

    own_pair.wait_recv()
    across_own = {}
    for k in ACROSS_FIRST:
        own_sum[k] = own_sum[k] + f32(own_pair_in[k])
        across_out[k] = bf16(own_sum[k, 1 - chip])
        across_own[k] = go(
            remote(across_out.at[k], across_own_in.at[k], across_send.at[k], across_recv.at[k], across)
        )
    for k in BACK_FIRST:
        own_sum[k] = own_sum[k] + f32(own_pair_in[k])

    back, across_in = {}, {}

    def later(k):
        arrived(k, 0)
        arrived(k, 1)
        pre = project(w_in.at[k], 0, 2, 4 * SUB, xv)
        arrived(k, 2)
        grad_hidden = project(w_in.at[k], 2, 1, 2 * SUB, cv)
        both, hidden = hidden_grads(pre, grad_hidden, 2)
        term = dot(both, xv[:, theirs], NN)
        in_pair_out[k, :, 0:2] = bf16(term).reshape(2, 2, SUB, half)
        term = dot(hidden, cv[:, theirs], NN)
        in_pair_out[k, :, 2:3] = bf16(term).reshape(2, 1, SUB, half)
        pair = go(remote(in_pair_out.at[k], in_pair_in.at[k], in_pair_send.at[k], in_pair_recv.at[k], sibling))
        term = dot(both, xv[:, mine], NN)
        in_sum[:, 0:2] = term.reshape(2, 2, SUB, half)
        term = dot(hidden, cv[:, mine], NN)
        in_sum[:, 2:3] = term.reshape(2, 1, SUB, half)
        pair.wait_recv()
        if k in BACK_FIRST:
            back_out[k] = bf16(in_sum[...] + f32(in_pair_in[k]))
            back[k] = go(remote(back_out.at[k], back_in.at[k], back_send.at[k], back_recv.at[k], down))
        else:
            other = 1 - down_chip
            across_in_out[k] = bf16(in_sum[other] + f32(in_pair_in[k, other]))
            across_in[k] = go(
                remote(across_in_out.at[k], across_in_in.at[k], across_in_send.at[k], across_in_recv.at[k], across)
            )
            in_keep[k] = in_sum[down_chip] + f32(in_pair_in[k, down_chip])

    in_keep = {}

    def section_sum(k):
        across_in[k].wait_recv()
        back_out[k, 0] = bf16(in_keep[k] + f32(across_in_in[k]))
        back[k] = go(remote(back_out.at[k, 0], back_in.at[k, 0], back_send.at[k], back_recv.at[k], down))

    def merge(k):
        back[k].wait_recv()
        across_out[k] = bf16(own_sum[k, 1 - chip] + f32(back_in[k, 1 - chip]))
        across_own[k] = go(
            remote(across_out.at[k], across_own_in.at[k], across_send.at[k], across_recv.at[k], across)
        )

    def finish(k):
        across_own[k].wait_recv()
        if k in BACK_FIRST:
            returned = back_in[k, chip]
        else:
            back[k].wait_recv()
            returned = back_in[k, 0]
        final[k] = bf16(own_sum[k, chip] + f32(returned) + f32(across_own_in[k]))
        owner = k // 2
        place = out_hbm.at[k % 2, :, :, mine]
        away = remote(final.at[k], place, fin_send.at[k], fin_recv.at[k], sibling)
        here = pltpu.make_async_copy(final.at[k], place, fin_send.at[k])

        @pl.when(core == owner)
        def _():
            here.start()

        @pl.when(core != owner)
        def _():
            away.start()

        def drain():
            @pl.when(core == owner)
            def _():
                here.wait()
                away.wait_recv()

            @pl.when(core != owner)
            def _():
                away.wait_send()

        return drain

    later(0)
    forward_relayed(1)
    later(1)
    forward(2)
    later(2)
    merge(0)
    section_sum(2)
    forward(3)
    later(3)
    merge(1)
    section_sum(3)
    drains = [finish(k) for k in (2, 0, 1, 3)]
    for copy in pending:
        copy.wait_send()
    for drain in drains:
        drain()


def per_device(n_blk, tokens, cotangent, gate_weight, up_weight, down_weight):
    tok, d = tokens.shape
    half = d // 2

    def cut(w):
        return w.reshape(2, CHUNKS, SUB, d)

    hbm = pl.BlockSpec(memory_space=pl.ANY)
    full = (CHUNKS, 2, 3, SUB, d)
    pair = (CHUNKS, 2, 3, SUB, half)
    one = (CHUNKS, 3, SUB, half)
    bf, fl = jnp.bfloat16, jnp.float32
    dma = pltpu.SemaphoreType.DMA
    out = pl.pallas_call(
        functools.partial(kernel, n_blk),
        out_shape=jax.ShapeDtypeStruct((2, 3, SUB, d), bf),
        in_specs=[hbm] * 5,
        out_specs=hbm,
        scratch_shapes=[
            pltpu.VMEM((tok, d), bf), pltpu.VMEM((tok, d), bf), pltpu.VMEM(full, bf), pltpu.VMEM(full, bf),
            pltpu.VMEM(pair, bf), pltpu.VMEM(pair, bf), pltpu.VMEM(pair, fl),
            pltpu.VMEM(pair, bf), pltpu.VMEM(pair, bf), pltpu.VMEM(pair[1:], fl),
            pltpu.VMEM(pair, bf), pltpu.VMEM(pair, bf),
            pltpu.VMEM(one, bf), pltpu.VMEM(one, bf), pltpu.VMEM(one, bf), pltpu.VMEM(one, bf), pltpu.VMEM(one, bf),
            dma((8,)),
            dma((CHUNKS, 3)), dma((CHUNKS, 3)), dma((CHUNKS, 3)), dma((CHUNKS, 3)),
            dma((CHUNKS, 3)), dma((CHUNKS, 3)), dma((CHUNKS, 3)), dma((CHUNKS, 3)),
            dma, dma, dma((CHUNKS,)), dma((CHUNKS,)),
            dma((CHUNKS,)), dma((CHUNKS,)), dma((CHUNKS,)), dma((CHUNKS,)),
            dma((CHUNKS,)), dma((CHUNKS,)), dma((CHUNKS,)), dma((CHUNKS,)),
        ],
        name="window",
        compiler_params=pltpu.CompilerParams(
            collective_id=0, has_side_effects=True, vmem_limit_bytes=58 << 20
        ),
    )(tokens, cotangent, cut(gate_weight), cut(up_weight), cut(down_weight))
    return tuple(out[:, m].reshape(2 * SUB, d) for m in range(3))


def solution(mesh):
    in_specs = (
        P(("blk", "dp"), None),
        P(("blk", "dp"), None),
        P("blk", None),
        P("blk", None),
        P("blk", None),
    )
    out_specs = (P(("blk", "dp"), None),) * 3
    return jax.shard_map(
        functools.partial(per_device, mesh.shape["blk"]),
        mesh=mesh, in_specs=in_specs, out_specs=out_specs, check_vma=False,
    )
```

```python
import functools

import jax
import jax.numpy as jnp
from jax import lax
from jax.experimental import pallas as pl
from jax.experimental.pallas import tpu as pltpu
from jax.sharding import PartitionSpec as P

MESH = pl.DeviceIdType.MESH
NT = (((1,), (1,)), ((), ()))
NN = (((1,), (0,)), ((), ()))
Z_LEN = 8
CHUNKS = 4
SUB = 16
RELAY = (0, 1)
DIRECT = (2, 3)
BACK_FIRST = (0, 1)
ACROSS_FIRST = (2, 3)
PIECES = (pl.ds(0, 1), pl.ds(1, 1), pl.ds(2, 1))


def dot(a, b, dims):
    return lax.dot_general(a, b, dims, preferred_element_type=jnp.float32)


def f32(v):
    return v.astype(jnp.float32)


def bf16(v):
    return v.astype(jnp.bfloat16)


def kernel(
    n_blk, x_hbm, c_hbm, wg_hbm, wu_hbm, wd_hbm, out_hbm,
    xv, cv, w_own, w_in,
    own_pair_out, own_pair_in, own_sum,
    in_pair_out, in_pair_in, in_sum,
    back_out, back_in, across_in_out, across_in_in, across_out, across_own_in, final,
    load_sem, up_send, up_recv, fwd_send, fwd_recv, relay_send, relay_recv, fwd2_send, fwd2_recv,
    own_pair_send, own_pair_recv, in_pair_send, in_pair_recv,
    back_send, back_recv, across_in_send, across_in_recv, across_send, across_recv, fin_send, fin_recv,
):
    j = lax.axis_index("blk")
    r = lax.axis_index("dp")
    chip = lax.div(r, 2)
    core = lax.rem(r, 2)
    place = lax.rem(j, Z_LEN)
    flip_up = jnp.where(place == Z_LEN - 1, 1, 0)
    flip_down = jnp.where(place == 0, 1, 0)
    up_chip = lax.rem(chip + flip_up, 2)
    down_chip = lax.rem(chip + flip_down, 2)
    up = (lax.rem(j + 1, n_blk), up_chip * 2 + core)
    down = (lax.rem(j + n_blk - 1, n_blk), down_chip * 2 + core)
    across = (j, (1 - chip) * 2 + core)
    sibling = (j, chip * 2 + 1 - core)
    half = xv.shape[1] // 2
    mine = pl.ds(pl.multiple_of(core * half, half), half)
    theirs = pl.ds(pl.multiple_of((1 - core) * half, half), half)
    w_hbm = (wg_hbm, wu_hbm, wd_hbm)

    def remote(src, dst, send, recv, device):
        return pltpu.make_async_remote_copy(
            src_ref=src, dst_ref=dst, send_sem=send, recv_sem=recv, device_id=device, device_id_type=MESH
        )

    loads = []
    for m in range(3):
        for p in range(2):
            loads.append(pltpu.make_async_copy(w_hbm[m].at[p], w_own.at[:, p, m], load_sem.at[m * 2 + p]))
    load_x = pltpu.make_async_copy(x_hbm, xv, load_sem.at[6])
    load_c = pltpu.make_async_copy(c_hbm, cv, load_sem.at[7])
    for load in loads[:4]:
        load.start()
    load_x.start()
    for load in loads[4:]:
        load.start()
    load_c.start()

    barrier = pltpu.get_barrier_semaphore()
    for device in (up, down, across, sibling):
        pl.semaphore_signal(barrier, inc=1, device_id=device, device_id_type=MESH)
    pl.semaphore_wait(barrier, 4)

    pending = []

    def go(copy):
        copy.start()
        pending.append(copy)
        return copy

    up_copies = {}
    for k in RELAY + DIRECT:
        for m in range(3):
            if k in RELAY:
                src, dst = w_hbm[m].at[up_chip, k, :, mine], w_in.at[k, up_chip, m, :, mine]
            else:
                src, dst = w_hbm[m].at[:, k, :, mine], w_in.at[k, :, m, :, mine]
            up_copies[k, m] = go(remote(src, dst, up_send.at[k, m], up_recv.at[k, m], up))

    fwd, relay, fwd2 = {}, {}, {}

    def forward(k, m):
        up_copies[k, m].wait_recv()
        if k in RELAY:
            piece = w_in.at[k, chip, m, :, mine]
            relay[k, m] = go(remote(piece, piece, relay_send.at[k, m], relay_recv.at[k, m], across))
        else:
            piece = w_in.at[k, :, m, :, mine]
        fwd[k, m] = go(remote(piece, piece, fwd_send.at[k, m], fwd_recv.at[k, m], sibling))

    def forward_relayed(k, m):
        relay[k, m].wait_recv()
        piece = w_in.at[k, 1 - chip, m, :, mine]
        fwd2[k, m] = go(remote(piece, piece, fwd2_send.at[k, m], fwd2_recv.at[k, m], sibling))

    def arrived(k, m):
        fwd[k, m].wait_recv()
        if k in RELAY:
            fwd2[k, m].wait_recv()

    def project(w, lo, n, rows, act):
        total = None
        for s in (pl.ds(0, half), pl.ds(half, half)):
            part = w[:, :, lo:lo + n, :, s] if len(w.shape) == 5 else w[:, lo:lo + n, :, s]
            term = dot(part.reshape(rows, half), act[:, s], NT)
            total = term if total is None else total + term
        return total

    def forward_parts(pre, groups):
        tok = pre.shape[-1]
        pre = pre.reshape(groups, 2, SUB, tok)
        gate, up_pre = pre[:, 0], pre[:, 1]
        squash = jax.nn.sigmoid(gate)
        silu = gate * squash
        hidden = bf16(silu * up_pre).reshape(groups * SUB, tok)
        slope = up_pre * squash * (1.0 + gate * (1.0 - squash))
        return hidden, slope, silu

    def backward_parts(grad_hidden, slope, silu, groups):
        tok = grad_hidden.shape[-1]
        grad_hidden = grad_hidden.reshape(groups, SUB, tok)
        both = jnp.stack([bf16(grad_hidden * slope), bf16(grad_hidden * silu)], axis=1)
        return both.reshape(groups * 2 * SUB, tok)

    own_groups = CHUNKS * 2
    for load in loads[:4]:
        load.wait()
    load_x.wait()
    pre = project(w_own, 0, 2, own_groups * 2 * SUB, xv)
    forward(0, 0)
    for load in loads[4:]:
        load.wait()
    load_c.wait()
    grad_hidden = project(w_own, 2, 1, own_groups * SUB, cv)
    forward(0, 1)
    hidden, slope, silu = forward_parts(pre, own_groups)
    both = backward_parts(grad_hidden, slope, silu, own_groups)
    term = dot(both, xv[:, theirs], NN)
    own_pair_out[:, :, 0:2] = bf16(term).reshape(CHUNKS, 2, 2, SUB, half)
    term = dot(hidden, cv[:, theirs], NN)
    own_pair_out[:, :, 2:3] = bf16(term).reshape(CHUNKS, 2, 1, SUB, half)
    own_pair = {}
    for g, ks in enumerate((ACROSS_FIRST, BACK_FIRST)):
        s = pl.ds(ks[0], len(ks))
        own_pair[g] = go(
            remote(own_pair_out.at[s], own_pair_in.at[s], own_pair_send.at[g], own_pair_recv.at[g], sibling)
        )
    forward(0, 2)
    term = dot(both, xv[:, mine], NN)
    own_sum[:, :, 0:2] = term.reshape(CHUNKS, 2, 2, SUB, half)
    forward_relayed(0, 0)
    forward_relayed(0, 1)
    term = dot(hidden, cv[:, mine], NN)
    own_sum[:, :, 2:3] = term.reshape(CHUNKS, 2, 1, SUB, half)
    forward_relayed(0, 2)
    forward(1, 0)

    across_own, across_in, back, pair, state = {}, {}, {}, {}, {}

    def own_chip_sums(g, ks):
        own_pair[g].wait_recv()
        for k in ks:
            own_sum[k] = own_sum[k] + f32(own_pair_in[k])

    def send_own(k):
        across_out[k] = bf16(own_sum[k, 1 - chip])
        across_own[k] = go(
            remote(across_out.at[k], across_own_in.at[k], across_send.at[k], across_recv.at[k], across)
        )

    def pair_send(k, n, s):
        pair[k, n] = go(
            remote(
                in_pair_out.at[k, :, s], in_pair_in.at[k, :, s], in_pair_send.at[k, n], in_pair_recv.at[k, n], sibling
            )
        )

    def down_terms(k):
        arrived(k, 0)
        arrived(k, 1)
        pre = project(w_in.at[k], 0, 2, 4 * SUB, xv)
        hidden, slope, silu = forward_parts(pre, 2)
        term = dot(hidden, cv[:, theirs], NN)
        in_pair_out[k, :, 2:3] = bf16(term).reshape(2, 1, SUB, half)
        pair_send(k, 1, pl.ds(2, 1))
        term = dot(hidden, cv[:, mine], NN)
        in_sum[k, :, 2:3] = term.reshape(2, 1, SUB, half)
        state[k] = slope, silu

    def back_project(k):
        arrived(k, 2)
        state[k] = backward_parts(project(w_in.at[k], 2, 1, 2 * SUB, cv), *state[k], 2)

    def gate_up_theirs(k):
        term = dot(state[k], xv[:, theirs], NN)
        in_pair_out[k, :, 0:2] = bf16(term).reshape(2, 2, SUB, half)
        pair_send(k, 0, pl.ds(0, 2))

    def gate_up_mine(k):
        term = dot(state[k], xv[:, mine], NN)
        in_sum[k, :, 0:2] = term.reshape(2, 2, SUB, half)

    def send_back(k):
        pair[k, 0].wait_recv()
        pair[k, 1].wait_recv()
        back_out[k] = bf16(in_sum[k] + f32(in_pair_in[k]))
        back[k, 0] = go(remote(back_out.at[k], back_in.at[k], back_send.at[k, 0], back_recv.at[k, 0], down))

    def send_across(k, n):
        if n != 1:
            pair[k, n // 2].wait_recv()
        s = PIECES[n]
        other = 1 - down_chip
        across_in_out[k, s] = bf16(in_sum[k, other, s] + f32(in_pair_in[k, other, s]))
        across_in[k, n] = go(
            remote(
                across_in_out.at[k, s], across_in_in.at[k, s], across_in_send.at[k, n], across_in_recv.at[k, n], across
            )
        )

    def section_sum(k, n):
        across_in[k, n].wait_recv()
        s = PIECES[n]
        total = in_sum[k, down_chip, s] + f32(in_pair_in[k, down_chip, s]) + f32(across_in_in[k, s])
        back_out[k, 0, s] = bf16(total)
        back[k, n] = go(
            remote(back_out.at[k, 0, s], back_in.at[k, 0, s], back_send.at[k, n], back_recv.at[k, n], down)
        )

    def merge(k):
        back[k, 0].wait_recv()
        across_out[k] = bf16(own_sum[k, 1 - chip] + f32(back_in[k, 1 - chip]))
        across_own[k] = go(
            remote(across_out.at[k], across_own_in.at[k], across_send.at[k], across_recv.at[k], across)
        )

    drains = []

    def write(k, n, s):
        owner = k // 2
        place = out_hbm.at[k % 2, s, :, mine]
        away = remote(final.at[k, s], place, fin_send.at[k, n], fin_recv.at[k, n], sibling)
        here = pltpu.make_async_copy(final.at[k, s], place, fin_send.at[k, n])

        @pl.when(core == owner)
        def _():
            here.start()

        @pl.when(core != owner)
        def _():
            away.start()

        def drain():
            @pl.when(core == owner)
            def _():
                here.wait()
                away.wait_recv()

            @pl.when(core != owner)
            def _():
                away.wait_send()

        drains.append(drain)

    def finish_back(k):
        across_own[k].wait_recv()
        final[k] = bf16(own_sum[k, chip] + f32(back_in[k, chip]) + f32(across_own_in[k]))
        write(k, 0, pl.ds(0, 3))

    def finish_across(k, n):
        if n == 2:
            across_own[k].wait_recv()
        back[k, n].wait_recv()
        s = PIECES[n]
        final[k, s] = bf16(own_sum[k, chip, s] + f32(back_in[k, 0, s]) + f32(across_own_in[k, s]))
        write(k, n, s)

    own_chip_sums(0, ACROSS_FIRST)
    down_terms(0)
    forward(1, 1)
    back_project(0)
    forward(1, 2)
    send_own(2)
    send_own(3)
    gate_up_theirs(0)
    forward_relayed(1, 0)
    forward_relayed(1, 1)
    gate_up_mine(0)
    forward_relayed(1, 2)
    own_chip_sums(1, BACK_FIRST)
    send_back(0)
    down_terms(1)
    back_project(1)
    gate_up_theirs(1)
    forward(2, 0)
    gate_up_mine(1)
    forward(2, 1)
    send_back(1)
    forward(2, 2)
    down_terms(2)
    back_project(2)
    gate_up_theirs(2)
    gate_up_mine(2)
    forward(3, 0)
    for n in (2, 0, 1):
        send_across(2, n)
    forward(3, 1)
    down_terms(3)
    merge(0)
    forward(3, 2)
    send_across(3, 2)
    back_project(3)
    gate_up_theirs(3)
    gate_up_mine(3)
    for n in (0, 1):
        send_across(3, n)
    for n in (2, 0, 1):
        section_sum(2, n)
    merge(1)
    for n in (2, 0, 1):
        section_sum(3, n)
    finish_back(0)
    for n in (2, 0, 1):
        finish_across(2, n)
    for n in (2, 0, 1):
        finish_across(3, n)
    finish_back(1)
    for copy in pending:
        copy.wait_send()
    for drain in drains:
        drain()


def per_device(n_blk, tokens, cotangent, gate_weight, up_weight, down_weight):
    tok, d = tokens.shape
    half = d // 2

    def cut(w):
        return w.reshape(2, CHUNKS, SUB, d)

    hbm = pl.BlockSpec(memory_space=pl.ANY)
    full = (CHUNKS, 2, 3, SUB, d)
    pair = (CHUNKS, 2, 3, SUB, half)
    one = (CHUNKS, 3, SUB, half)
    bf, fl = jnp.bfloat16, jnp.float32
    dma = pltpu.SemaphoreType.DMA
    out = pl.pallas_call(
        functools.partial(kernel, n_blk),
        out_shape=jax.ShapeDtypeStruct((2, 3, SUB, d), bf),
        in_specs=[hbm] * 5,
        out_specs=hbm,
        scratch_shapes=[
            pltpu.VMEM((tok, d), bf), pltpu.VMEM((tok, d), bf), pltpu.VMEM(full, bf), pltpu.VMEM(full, bf),
            pltpu.VMEM(pair, bf), pltpu.VMEM(pair, bf), pltpu.VMEM(pair, fl),
            pltpu.VMEM(pair, bf), pltpu.VMEM(pair, bf), pltpu.VMEM(pair, fl),
            pltpu.VMEM(pair, bf), pltpu.VMEM(pair, bf),
            pltpu.VMEM(one, bf), pltpu.VMEM(one, bf), pltpu.VMEM(one, bf), pltpu.VMEM(one, bf), pltpu.VMEM(one, bf),
            dma((8,)),
            dma((CHUNKS, 3)), dma((CHUNKS, 3)), dma((CHUNKS, 3)), dma((CHUNKS, 3)),
            dma((CHUNKS, 3)), dma((CHUNKS, 3)), dma((CHUNKS, 3)), dma((CHUNKS, 3)),
            dma((2,)), dma((2,)), dma((CHUNKS, 2)), dma((CHUNKS, 2)),
            dma((CHUNKS, 3)), dma((CHUNKS, 3)), dma((CHUNKS, 3)), dma((CHUNKS, 3)),
            dma((CHUNKS,)), dma((CHUNKS,)), dma((CHUNKS, 3)), dma((CHUNKS, 3)),
        ],
        name="window",
        compiler_params=pltpu.CompilerParams(
            collective_id=0, has_side_effects=True, vmem_limit_bytes=58 << 20
        ),
    )(tokens, cotangent, cut(gate_weight), cut(up_weight), cut(down_weight))
    return tuple(out[:, m].reshape(2 * SUB, d) for m in range(3))


def solution(mesh):
    in_specs = (
        P(("blk", "dp"), None),
        P(("blk", "dp"), None),
        P("blk", None),
        P("blk", None),
        P("blk", None),
    )
    out_specs = (P(("blk", "dp"), None),) * 3
    return jax.shard_map(
        functools.partial(per_device, mesh.shape["blk"]),
        mesh=mesh, in_specs=in_specs, out_specs=out_specs, check_vma=False,
    )
```

```python
import functools

import jax
import jax.numpy as jnp
from jax import lax
from jax.experimental import pallas as pl
from jax.experimental.pallas import tpu as pltpu
from jax.sharding import PartitionSpec as P

MESH = pl.DeviceIdType.MESH
NT = (((1,), (1,)), ((), ()))
NN = (((1,), (0,)), ((), ()))
Z_LEN = 8
CHUNKS = 4
SUB = 16
RELAY = (0, 1)
DIRECT = (2, 3)
BACK_FIRST = (0, 1)
ACROSS_FIRST = (2, 3)
PIECES = (pl.ds(0, 1), pl.ds(1, 1), pl.ds(2, 1))


def dot(a, b, dims):
    return lax.dot_general(a, b, dims, preferred_element_type=jnp.float32)


def f32(v):
    return v.astype(jnp.float32)


def bf16(v):
    return v.astype(jnp.bfloat16)


def kernel(
    n_blk, x_hbm, c_hbm, wg_hbm, wu_hbm, wd_hbm, out_hbm,
    xv, cv, w_own, w_in,
    own_pair_out, own_pair_in, own_sum,
    in_pair_out, in_pair_in, in_sum,
    back_out, back_in, across_in_out, across_in_in, across_out, across_own_in, final,
    load_sem, up_send, up_recv, fwd_send, fwd_recv, relay_send, relay_recv, fwd2_send, fwd2_recv,
    own_pair_send, own_pair_recv, in_pair_send, in_pair_recv,
    back_send, back_recv, across_in_send, across_in_recv, across_send, across_recv, fin_send, fin_recv,
):
    j = lax.axis_index("blk")
    r = lax.axis_index("dp")
    chip = lax.div(r, 2)
    core = lax.rem(r, 2)
    place = lax.rem(j, Z_LEN)
    flip_up = jnp.where(place == Z_LEN - 1, 1, 0)
    flip_down = jnp.where(place == 0, 1, 0)
    up_chip = lax.rem(chip + flip_up, 2)
    down_chip = lax.rem(chip + flip_down, 2)
    up = (lax.rem(j + 1, n_blk), up_chip * 2 + core)
    down = (lax.rem(j + n_blk - 1, n_blk), down_chip * 2 + core)
    across = (j, (1 - chip) * 2 + core)
    sibling = (j, chip * 2 + 1 - core)
    half = xv.shape[1] // 2
    mine = pl.ds(pl.multiple_of(core * half, half), half)
    theirs = pl.ds(pl.multiple_of((1 - core) * half, half), half)
    w_hbm = (wg_hbm, wu_hbm, wd_hbm)

    def remote(src, dst, send, recv, device):
        return pltpu.make_async_remote_copy(
            src_ref=src, dst_ref=dst, send_sem=send, recv_sem=recv, device_id=device, device_id_type=MESH
        )

    loads = []
    for m in range(3):
        for p in range(2):
            loads.append(pltpu.make_async_copy(w_hbm[m].at[p], w_own.at[:, p, m], load_sem.at[m * 2 + p]))
    load_x = pltpu.make_async_copy(x_hbm, xv, load_sem.at[6])
    load_c = pltpu.make_async_copy(c_hbm, cv, load_sem.at[7])
    for load in loads[:4]:
        load.start()
    load_x.start()
    for load in loads[4:]:
        load.start()
    load_c.start()

    barrier = pltpu.get_barrier_semaphore()
    for device in (up, down, across, sibling):
        pl.semaphore_signal(barrier, inc=1, device_id=device, device_id_type=MESH)
    pl.semaphore_wait(barrier, 4)

    pending = []

    def go(copy):
        copy.start()
        pending.append(copy)
        return copy

    up_copies = {}
    for k in RELAY + DIRECT:
        for m in range(3):
            if k in RELAY:
                src, dst = w_hbm[m].at[up_chip, k, :, mine], w_in.at[k, up_chip, m, :, mine]
            else:
                src, dst = w_hbm[m].at[:, k, :, mine], w_in.at[k, :, m, :, mine]
            up_copies[k, m] = go(remote(src, dst, up_send.at[k, m], up_recv.at[k, m], up))

    fwd, relay, fwd2 = {}, {}, {}

    def forward(k, m):
        up_copies[k, m].wait_recv()
        if k in RELAY:
            piece = w_in.at[k, chip, m, :, mine]
            relay[k, m] = go(remote(piece, piece, relay_send.at[k, m], relay_recv.at[k, m], across))
        else:
            piece = w_in.at[k, :, m, :, mine]
        fwd[k, m] = go(remote(piece, piece, fwd_send.at[k, m], fwd_recv.at[k, m], sibling))

    def forward_relayed(k, m):
        relay[k, m].wait_recv()
        piece = w_in.at[k, 1 - chip, m, :, mine]
        fwd2[k, m] = go(remote(piece, piece, fwd2_send.at[k, m], fwd2_recv.at[k, m], sibling))

    def arrived(k, m):
        fwd[k, m].wait_recv()
        if k in RELAY:
            fwd2[k, m].wait_recv()

    def project(w, lo, n, rows, act):
        total = None
        for s in (pl.ds(0, half), pl.ds(half, half)):
            part = w[:, :, lo:lo + n, :, s] if len(w.shape) == 5 else w[:, lo:lo + n, :, s]
            term = dot(part.reshape(rows, half), act[:, s], NT)
            total = term if total is None else total + term
        return total

    def forward_parts(pre, groups):
        tok = pre.shape[-1]
        pre = pre.reshape(groups, 2, SUB, tok)
        gate, up_pre = pre[:, 0], pre[:, 1]
        squash = jax.nn.sigmoid(gate)
        silu = gate * squash
        hidden = bf16(silu * up_pre).reshape(groups * SUB, tok)
        slope = up_pre * squash * (1.0 + gate * (1.0 - squash))
        return hidden, slope, silu

    def backward_parts(grad_hidden, slope, silu, groups):
        tok = grad_hidden.shape[-1]
        grad_hidden = grad_hidden.reshape(groups, SUB, tok)
        both = jnp.stack([bf16(grad_hidden * slope), bf16(grad_hidden * silu)], axis=1)
        return both.reshape(groups * 2 * SUB, tok)

    own_groups = CHUNKS * 2
    for load in loads[:4]:
        load.wait()
    load_x.wait()
    pre = project(w_own, 0, 2, own_groups * 2 * SUB, xv)
    forward(0, 0)
    for load in loads[4:]:
        load.wait()
    load_c.wait()
    grad_hidden = project(w_own, 2, 1, own_groups * SUB, cv)
    forward(0, 1)
    hidden, slope, silu = forward_parts(pre, own_groups)
    both = backward_parts(grad_hidden, slope, silu, own_groups)
    term = dot(both, xv[:, theirs], NN)
    own_pair_out[:, :, 0:2] = bf16(term).reshape(CHUNKS, 2, 2, SUB, half)
    term = dot(hidden, cv[:, theirs], NN)
    own_pair_out[:, :, 2:3] = bf16(term).reshape(CHUNKS, 2, 1, SUB, half)
    forward(0, 2)
    term = dot(both, xv[:, mine], NN)
    own_sum[:, :, 0:2] = term.reshape(CHUNKS, 2, 2, SUB, half)
    forward_relayed(0, 0)
    forward_relayed(0, 1)
    term = dot(hidden, cv[:, mine], NN)
    own_sum[:, :, 2:3] = term.reshape(CHUNKS, 2, 1, SUB, half)
    forward_relayed(0, 2)
    own_pair = {}
    for g, ks in enumerate((ACROSS_FIRST, BACK_FIRST)):
        s = pl.ds(ks[0], len(ks))
        own_pair[g] = go(
            remote(own_pair_out.at[s], own_pair_in.at[s], own_pair_send.at[g], own_pair_recv.at[g], sibling)
        )
    forward(1, 0)
    forward(1, 1)

    across_own, across_in, back, pair, state = {}, {}, {}, {}, {}

    def own_chip_sums(g, ks):
        own_pair[g].wait_recv()
        for k in ks:
            own_sum[k] = own_sum[k] + f32(own_pair_in[k])

    def send_own(k):
        across_out[k] = bf16(own_sum[k, 1 - chip])
        across_own[k] = go(
            remote(across_out.at[k], across_own_in.at[k], across_send.at[k], across_recv.at[k], across)
        )

    def pair_send(k, n, s):
        pair[k, n] = go(
            remote(
                in_pair_out.at[k, :, s], in_pair_in.at[k, :, s], in_pair_send.at[k, n], in_pair_recv.at[k, n], sibling
            )
        )

    def down_terms(k):
        arrived(k, 0)
        arrived(k, 1)
        pre = project(w_in.at[k], 0, 2, 4 * SUB, xv)
        hidden, slope, silu = forward_parts(pre, 2)
        term = dot(hidden, cv[:, theirs], NN)
        in_pair_out[k, :, 2:3] = bf16(term).reshape(2, 1, SUB, half)
        pair_send(k, 1, pl.ds(2, 1))
        term = dot(hidden, cv[:, mine], NN)
        in_sum[k, :, 2:3] = term.reshape(2, 1, SUB, half)
        state[k] = slope, silu

    def back_project(k):
        arrived(k, 2)
        state[k] = backward_parts(project(w_in.at[k], 2, 1, 2 * SUB, cv), *state[k], 2)

    def gate_up_theirs(k):
        term = dot(state[k], xv[:, theirs], NN)
        in_pair_out[k, :, 0:2] = bf16(term).reshape(2, 2, SUB, half)
        pair_send(k, 0, pl.ds(0, 2))

    def gate_up_mine(k):
        term = dot(state[k], xv[:, mine], NN)
        in_sum[k, :, 0:2] = term.reshape(2, 2, SUB, half)

    def send_back(k):
        pair[k, 0].wait_recv()
        pair[k, 1].wait_recv()
        back_out[k] = bf16(in_sum[k] + f32(in_pair_in[k]))
        back[k, 0] = go(remote(back_out.at[k], back_in.at[k], back_send.at[k, 0], back_recv.at[k, 0], down))

    def send_across(k, n):
        if n != 1:
            pair[k, n // 2].wait_recv()
        s = PIECES[n]
        other = 1 - down_chip
        across_in_out[k, s] = bf16(in_sum[k, other, s] + f32(in_pair_in[k, other, s]))
        across_in[k, n] = go(
            remote(
                across_in_out.at[k, s], across_in_in.at[k, s], across_in_send.at[k, n], across_in_recv.at[k, n], across
            )
        )

    def section_sum(k, n):
        across_in[k, n].wait_recv()
        s = PIECES[n]
        total = in_sum[k, down_chip, s] + f32(in_pair_in[k, down_chip, s]) + f32(across_in_in[k, s])
        back_out[k, 0, s] = bf16(total)
        back[k, n] = go(
            remote(back_out.at[k, 0, s], back_in.at[k, 0, s], back_send.at[k, n], back_recv.at[k, n], down)
        )

    def merge(k):
        back[k, 0].wait_recv()
        across_out[k] = bf16(own_sum[k, 1 - chip] + f32(back_in[k, 1 - chip]))
        across_own[k] = go(
            remote(across_out.at[k], across_own_in.at[k], across_send.at[k], across_recv.at[k], across)
        )

    drains = []

    def write(k, n, s):
        owner = k // 2
        place = out_hbm.at[s, k % 2, :, mine]
        away = remote(final.at[k, s], place, fin_send.at[k, n], fin_recv.at[k, n], sibling)
        here = pltpu.make_async_copy(final.at[k, s], place, fin_send.at[k, n])

        @pl.when(core == owner)
        def _():
            here.start()

        @pl.when(core != owner)
        def _():
            away.start()

        def drain():
            @pl.when(core == owner)
            def _():
                here.wait()
                away.wait_recv()

            @pl.when(core != owner)
            def _():
                away.wait_send()

        drains.append(drain)

    def finish_back(k):
        across_own[k].wait_recv()
        final[k] = bf16(own_sum[k, chip] + f32(back_in[k, chip]) + f32(across_own_in[k]))
        write(k, 0, pl.ds(0, 3))

    def finish_across(k, n):
        if n == 2:
            across_own[k].wait_recv()
        back[k, n].wait_recv()
        s = PIECES[n]
        final[k, s] = bf16(own_sum[k, chip, s] + f32(back_in[k, 0, s]) + f32(across_own_in[k, s]))
        write(k, n, s)

    down_terms(0)
    forward(1, 2)
    back_project(0)
    gate_up_theirs(0)
    own_chip_sums(0, ACROSS_FIRST)
    send_own(2)
    send_own(3)
    gate_up_mine(0)
    forward_relayed(1, 0)
    forward_relayed(1, 1)
    send_back(0)
    forward_relayed(1, 2)
    forward(2, 0)
    own_chip_sums(1, BACK_FIRST)
    down_terms(1)
    forward(2, 1)
    back_project(1)
    gate_up_theirs(1)
    forward(2, 2)
    gate_up_mine(1)
    send_back(1)
    down_terms(2)
    back_project(2)
    gate_up_theirs(2)
    forward(3, 0)
    gate_up_mine(2)
    for n in (2, 0, 1):
        send_across(2, n)
    merge(0)
    forward(3, 1)
    down_terms(3)
    forward(3, 2)
    send_across(3, 2)
    back_project(3)
    gate_up_theirs(3)
    for n in (2, 0, 1):
        section_sum(2, n)
    gate_up_mine(3)
    for n in (0, 1):
        send_across(3, n)
    merge(1)
    for n in (2, 0, 1):
        section_sum(3, n)
    finish_back(0)
    for n in (2, 0, 1):
        finish_across(2, n)
    for n in (2, 0, 1):
        finish_across(3, n)
    finish_back(1)
    for copy in pending:
        copy.wait_send()
    for drain in drains:
        drain()


def per_device(n_blk, tokens, cotangent, gate_weight, up_weight, down_weight):
    tok, d = tokens.shape
    half = d // 2

    def cut(w):
        return w.reshape(2, CHUNKS, SUB, d)

    hbm = pl.BlockSpec(memory_space=pl.ANY)
    full = (CHUNKS, 2, 3, SUB, d)
    pair = (CHUNKS, 2, 3, SUB, half)
    one = (CHUNKS, 3, SUB, half)
    bf, fl = jnp.bfloat16, jnp.float32
    dma = pltpu.SemaphoreType.DMA
    out = pl.pallas_call(
        functools.partial(kernel, n_blk),
        out_shape=jax.ShapeDtypeStruct((3, 2, SUB, d), bf),
        in_specs=[hbm] * 5,
        out_specs=hbm,
        scratch_shapes=[
            pltpu.VMEM((tok, d), bf), pltpu.VMEM((tok, d), bf), pltpu.VMEM(full, bf), pltpu.VMEM(full, bf),
            pltpu.VMEM(pair, bf), pltpu.VMEM(pair, bf), pltpu.VMEM(pair, fl),
            pltpu.VMEM(pair, bf), pltpu.VMEM(pair, bf), pltpu.VMEM(pair, fl),
            pltpu.VMEM(pair, bf), pltpu.VMEM(pair, bf),
            pltpu.VMEM(one, bf), pltpu.VMEM(one, bf), pltpu.VMEM(one, bf), pltpu.VMEM(one, bf), pltpu.VMEM(one, bf),
            dma((8,)),
            dma((CHUNKS, 3)), dma((CHUNKS, 3)), dma((CHUNKS, 3)), dma((CHUNKS, 3)),
            dma((CHUNKS, 3)), dma((CHUNKS, 3)), dma((CHUNKS, 3)), dma((CHUNKS, 3)),
            dma((2,)), dma((2,)), dma((CHUNKS, 2)), dma((CHUNKS, 2)),
            dma((CHUNKS, 3)), dma((CHUNKS, 3)), dma((CHUNKS, 3)), dma((CHUNKS, 3)),
            dma((CHUNKS,)), dma((CHUNKS,)), dma((CHUNKS, 3)), dma((CHUNKS, 3)),
        ],
        name="window",
        compiler_params=pltpu.CompilerParams(
            collective_id=0, has_side_effects=True, vmem_limit_bytes=58 << 20
        ),
    )(tokens, cotangent, cut(gate_weight), cut(up_weight), cut(down_weight))
    return tuple(out[m].reshape(2 * SUB, d) for m in range(3))


def solution(mesh):
    in_specs = (
        P(("blk", "dp"), None),
        P(("blk", "dp"), None),
        P("blk", None),
        P("blk", None),
        P("blk", None),
    )
    out_specs = (P(("blk", "dp"), None),) * 3
    return jax.shard_map(
        functools.partial(per_device, mesh.shape["blk"]),
        mesh=mesh, in_specs=in_specs, out_specs=out_specs, check_vma=False,
    )
```

```python
import functools

import jax
import jax.numpy as jnp
from jax import lax
from jax.experimental import pallas as pl
from jax.experimental.pallas import tpu as pltpu
from jax.sharding import PartitionSpec as P

MESH = pl.DeviceIdType.MESH
NT = (((1,), (1,)), ((), ()))
NN = (((1,), (0,)), ((), ()))
Z_LEN = 8
CHUNKS = 4
SUB = 16
RELAY = (0, 1)
DIRECT = (2, 3)
BACK_FIRST = (0, 1)
ACROSS_FIRST = (2, 3)
PIECES = (pl.ds(0, 1), pl.ds(1, 1), pl.ds(2, 1))


def dot(a, b, dims):
    return lax.dot_general(a, b, dims, preferred_element_type=jnp.float32)


def f32(v):
    return v.astype(jnp.float32)


def bf16(v):
    return v.astype(jnp.bfloat16)


def kernel(
    n_blk, x_hbm, c_hbm, wg_hbm, wu_hbm, wd_hbm, out_hbm,
    xv, cv, w_own, w_in,
    own_pair_out, own_pair_in, own_sum,
    in_pair_out, in_pair_in, in_sum,
    back_out, back_in, across_in_out, across_in_in, across_out, across_own_in, final,
    load_sem, up_send, up_recv, fwd_send, fwd_recv, relay_send, relay_recv, fwd2_send, fwd2_recv,
    own_pair_send, own_pair_recv, in_pair_send, in_pair_recv,
    back_send, back_recv, across_in_send, across_in_recv, across_send, across_recv, fin_send, fin_recv,
):
    j = lax.axis_index("blk")
    r = lax.axis_index("dp")
    chip = lax.div(r, 2)
    core = lax.rem(r, 2)
    place = lax.rem(j, Z_LEN)
    flip_up = jnp.where(place == Z_LEN - 1, 1, 0)
    flip_down = jnp.where(place == 0, 1, 0)
    up_chip = lax.rem(chip + flip_up, 2)
    down_chip = lax.rem(chip + flip_down, 2)
    up = (lax.rem(j + 1, n_blk), up_chip * 2 + core)
    down = (lax.rem(j + n_blk - 1, n_blk), down_chip * 2 + core)
    across = (j, (1 - chip) * 2 + core)
    sibling = (j, chip * 2 + 1 - core)
    half = xv.shape[1] // 2
    mine = pl.ds(pl.multiple_of(core * half, half), half)
    theirs = pl.ds(pl.multiple_of((1 - core) * half, half), half)
    w_hbm = (wg_hbm, wu_hbm, wd_hbm)

    def remote(src, dst, send, recv, device):
        return pltpu.make_async_remote_copy(
            src_ref=src, dst_ref=dst, send_sem=send, recv_sem=recv, device_id=device, device_id_type=MESH
        )

    loads = []
    for m in range(3):
        for p in range(2):
            loads.append(pltpu.make_async_copy(w_hbm[m].at[p], w_own.at[:, p, m], load_sem.at[m * 2 + p]))
    load_x = pltpu.make_async_copy(x_hbm, xv, load_sem.at[6])
    load_c = pltpu.make_async_copy(c_hbm, cv, load_sem.at[7])
    for load in loads[:4]:
        load.start()
    load_x.start()
    for load in loads[4:]:
        load.start()
    load_c.start()

    barrier = pltpu.get_barrier_semaphore()
    for device in (up, down, across, sibling):
        pl.semaphore_signal(barrier, inc=1, device_id=device, device_id_type=MESH)
    pl.semaphore_wait(barrier, 4)

    pending = []

    def go(copy):
        copy.start()
        pending.append(copy)
        return copy

    up_copies = {}
    for k in RELAY + DIRECT:
        for m in range(3):
            if k in RELAY:
                src, dst = w_hbm[m].at[up_chip, k, :, mine], w_in.at[k, up_chip, m, :, mine]
            else:
                src, dst = w_hbm[m].at[:, k, :, mine], w_in.at[k, :, m, :, mine]
            up_copies[k, m] = go(remote(src, dst, up_send.at[k, m], up_recv.at[k, m], up))

    fwd, relay, fwd2 = {}, {}, {}

    def forward(k, m):
        up_copies[k, m].wait_recv()
        if k in RELAY:
            piece = w_in.at[k, chip, m, :, mine]
            relay[k, m] = go(remote(piece, piece, relay_send.at[k, m], relay_recv.at[k, m], across))
        else:
            piece = w_in.at[k, :, m, :, mine]
        fwd[k, m] = go(remote(piece, piece, fwd_send.at[k, m], fwd_recv.at[k, m], sibling))

    def forward_relayed(k, m):
        relay[k, m].wait_recv()
        piece = w_in.at[k, 1 - chip, m, :, mine]
        fwd2[k, m] = go(remote(piece, piece, fwd2_send.at[k, m], fwd2_recv.at[k, m], sibling))

    def arrived(k, m):
        fwd[k, m].wait_recv()
        if k in RELAY:
            fwd2[k, m].wait_recv()

    def project(w, lo, n, rows, act):
        total = None
        for s in (pl.ds(0, half), pl.ds(half, half)):
            part = w[:, :, lo:lo + n, :, s] if len(w.shape) == 5 else w[:, lo:lo + n, :, s]
            term = dot(part.reshape(rows, half), act[:, s], NT)
            total = term if total is None else total + term
        return total

    def forward_parts(pre, groups):
        tok = pre.shape[-1]
        pre = pre.reshape(groups, 2, SUB, tok)
        gate, up_pre = pre[:, 0], pre[:, 1]
        squash = jax.nn.sigmoid(gate)
        silu = gate * squash
        hidden = bf16(silu * up_pre).reshape(groups * SUB, tok)
        slope = up_pre * squash * (1.0 + gate * (1.0 - squash))
        return hidden, slope, silu

    def backward_parts(grad_hidden, slope, silu, groups):
        tok = grad_hidden.shape[-1]
        grad_hidden = grad_hidden.reshape(groups, SUB, tok)
        both = jnp.stack([bf16(grad_hidden * slope), bf16(grad_hidden * silu)], axis=1)
        return both.reshape(groups * 2 * SUB, tok)

    own_groups = CHUNKS * 2
    for load in loads[:4]:
        load.wait()
    load_x.wait()
    pre = project(w_own, 0, 2, own_groups * 2 * SUB, xv)
    forward(0, 0)
    for load in loads[4:]:
        load.wait()
    load_c.wait()
    grad_hidden = project(w_own, 2, 1, own_groups * SUB, cv)
    forward(0, 1)
    hidden, slope, silu = forward_parts(pre, own_groups)
    both = backward_parts(grad_hidden, slope, silu, own_groups)
    term = dot(both, xv[:, theirs], NN)
    own_pair_out[:, :, 0:2] = bf16(term).reshape(CHUNKS, 2, 2, SUB, half)
    term = dot(hidden, cv[:, theirs], NN)
    own_pair_out[:, :, 2:3] = bf16(term).reshape(CHUNKS, 2, 1, SUB, half)
    forward(0, 2)
    term = dot(both, xv[:, mine], NN)
    own_sum[:, :, 0:2] = term.reshape(CHUNKS, 2, 2, SUB, half)
    forward_relayed(0, 0)
    forward_relayed(0, 1)
    term = dot(hidden, cv[:, mine], NN)
    own_sum[:, :, 2:3] = term.reshape(CHUNKS, 2, 1, SUB, half)
    forward_relayed(0, 2)
    own_pair = {}
    for g, ks in enumerate((ACROSS_FIRST, BACK_FIRST)):
        s = pl.ds(ks[0], len(ks))
        own_pair[g] = go(
            remote(own_pair_out.at[s], own_pair_in.at[s], own_pair_send.at[g], own_pair_recv.at[g], sibling)
        )
    forward(1, 0)
    forward(1, 1)

    across_own, across_in, back, pair, state = {}, {}, {}, {}, {}

    def own_chip_sums(g, ks):
        own_pair[g].wait_recv()
        for k in ks:
            own_sum[k] = own_sum[k] + f32(own_pair_in[k])

    def send_own(k):
        across_out[k] = bf16(own_sum[k, 1 - chip])
        across_own[k] = go(
            remote(across_out.at[k], across_own_in.at[k], across_send.at[k], across_recv.at[k], across)
        )

    def pair_send(k, n, s):
        pair[k, n] = go(
            remote(
                in_pair_out.at[k, :, s], in_pair_in.at[k, :, s], in_pair_send.at[k, n], in_pair_recv.at[k, n], sibling
            )
        )

    def down_terms(k):
        arrived(k, 0)
        arrived(k, 1)
        pre = project(w_in.at[k], 0, 2, 4 * SUB, xv)
        hidden, slope, silu = forward_parts(pre, 2)
        term = dot(hidden, cv[:, theirs], NN)
        in_pair_out[k, :, 2:3] = bf16(term).reshape(2, 1, SUB, half)
        pair_send(k, 1, pl.ds(2, 1))
        term = dot(hidden, cv[:, mine], NN)
        in_sum[k, :, 2:3] = term.reshape(2, 1, SUB, half)
        state[k] = slope, silu

    def back_project(k):
        arrived(k, 2)
        state[k] = backward_parts(project(w_in.at[k], 2, 1, 2 * SUB, cv), *state[k], 2)

    def gate_up_theirs(k):
        term = dot(state[k], xv[:, theirs], NN)
        in_pair_out[k, :, 0:2] = bf16(term).reshape(2, 2, SUB, half)
        pair_send(k, 0, pl.ds(0, 2))

    def gate_up_mine(k):
        term = dot(state[k], xv[:, mine], NN)
        in_sum[k, :, 0:2] = term.reshape(2, 2, SUB, half)

    def send_back(k):
        pair[k, 0].wait_recv()
        pair[k, 1].wait_recv()
        back_out[k] = bf16(in_sum[k] + f32(in_pair_in[k]))
        back[k, 0] = go(remote(back_out.at[k], back_in.at[k], back_send.at[k, 0], back_recv.at[k, 0], down))

    def send_across(k, n):
        if n != 1:
            pair[k, n // 2].wait_recv()
        s = PIECES[n]
        other = 1 - down_chip
        across_in_out[k, s] = bf16(in_sum[k, other, s] + f32(in_pair_in[k, other, s]))
        across_in[k, n] = go(
            remote(
                across_in_out.at[k, s], across_in_in.at[k, s], across_in_send.at[k, n], across_in_recv.at[k, n], across
            )
        )

    def section_sum(k, n):
        across_in[k, n].wait_recv()
        s = PIECES[n]
        total = in_sum[k, down_chip, s] + f32(in_pair_in[k, down_chip, s]) + f32(across_in_in[k, s])
        back_out[k, 0, s] = bf16(total)
        back[k, n] = go(
            remote(back_out.at[k, 0, s], back_in.at[k, 0, s], back_send.at[k, n], back_recv.at[k, n], down)
        )

    def merge(k):
        back[k, 0].wait_recv()
        across_out[k] = bf16(own_sum[k, 1 - chip] + f32(back_in[k, 1 - chip]))
        across_own[k] = go(
            remote(across_out.at[k], across_own_in.at[k], across_send.at[k], across_recv.at[k], across)
        )

    drains = []

    def write(k, n, s):
        owner = k // 2
        place = out_hbm.at[s, k % 2, :, mine]
        away = remote(final.at[k, s], place, fin_send.at[k, n], fin_recv.at[k, n], sibling)
        here = pltpu.make_async_copy(final.at[k, s], place, fin_send.at[k, n])

        @pl.when(core == owner)
        def _():
            here.start()

        @pl.when(core != owner)
        def _():
            away.start()

        def drain():
            @pl.when(core == owner)
            def _():
                here.wait()
                away.wait_recv()

            @pl.when(core != owner)
            def _():
                away.wait_send()

        drains.append(drain)

    def finish_back(k):
        across_own[k].wait_recv()
        final[k] = bf16(own_sum[k, chip] + f32(back_in[k, chip]) + f32(across_own_in[k]))
        write(k, 0, pl.ds(0, 3))

    def finish_across(k, n):
        if n == 2:
            across_own[k].wait_recv()
        back[k, n].wait_recv()
        s = PIECES[n]
        final[k, s] = bf16(own_sum[k, chip, s] + f32(back_in[k, 0, s]) + f32(across_own_in[k, s]))
        write(k, n, s)

    down_terms(0)
    forward(1, 2)
    back_project(0)
    gate_up_theirs(0)
    own_chip_sums(0, ACROSS_FIRST)
    send_own(2)
    send_own(3)
    gate_up_mine(0)
    forward_relayed(1, 0)
    forward_relayed(1, 1)
    send_back(0)
    forward_relayed(1, 2)
    forward(2, 0)
    own_chip_sums(1, BACK_FIRST)
    down_terms(1)
    forward(2, 1)
    back_project(1)
    gate_up_theirs(1)
    forward(2, 2)
    gate_up_mine(1)
    send_back(1)
    down_terms(2)
    back_project(2)
    gate_up_theirs(2)
    forward(3, 0)
    gate_up_mine(2)
    for n in (2, 0, 1):
        send_across(2, n)
    merge(0)
    forward(3, 1)
    down_terms(3)
    forward(3, 2)
    send_across(3, 2)
    back_project(3)
    gate_up_theirs(3)
    for n in (2, 0, 1):
        section_sum(2, n)
    gate_up_mine(3)
    for n in (0, 1):
        send_across(3, n)
    merge(1)
    section_sum(3, 2)
    finish_back(0)
    for n in (0, 1):
        section_sum(3, n)
    for n in (2, 0, 1):
        finish_across(2, n)
    for n in (2, 0, 1):
        finish_across(3, n)
    finish_back(1)
    for copy in pending:
        copy.wait_send()
    for drain in drains:
        drain()


def per_device(n_blk, tokens, cotangent, gate_weight, up_weight, down_weight):
    tok, d = tokens.shape
    half = d // 2

    def cut(w):
        return w.reshape(2, CHUNKS, SUB, d)

    hbm = pl.BlockSpec(memory_space=pl.ANY)
    full = (CHUNKS, 2, 3, SUB, d)
    pair = (CHUNKS, 2, 3, SUB, half)
    one = (CHUNKS, 3, SUB, half)
    bf, fl = jnp.bfloat16, jnp.float32
    dma = pltpu.SemaphoreType.DMA
    out = pl.pallas_call(
        functools.partial(kernel, n_blk),
        out_shape=jax.ShapeDtypeStruct((3, 2, SUB, d), bf),
        in_specs=[hbm] * 5,
        out_specs=hbm,
        scratch_shapes=[
            pltpu.VMEM((tok, d), bf), pltpu.VMEM((tok, d), bf), pltpu.VMEM(full, bf), pltpu.VMEM(full, bf),
            pltpu.VMEM(pair, bf), pltpu.VMEM(pair, bf), pltpu.VMEM(pair, fl),
            pltpu.VMEM(pair, bf), pltpu.VMEM(pair, bf), pltpu.VMEM(pair, fl),
            pltpu.VMEM(pair, bf), pltpu.VMEM(pair, bf),
            pltpu.VMEM(one, bf), pltpu.VMEM(one, bf), pltpu.VMEM(one, bf), pltpu.VMEM(one, bf), pltpu.VMEM(one, bf),
            dma((8,)),
            dma((CHUNKS, 3)), dma((CHUNKS, 3)), dma((CHUNKS, 3)), dma((CHUNKS, 3)),
            dma((CHUNKS, 3)), dma((CHUNKS, 3)), dma((CHUNKS, 3)), dma((CHUNKS, 3)),
            dma((2,)), dma((2,)), dma((CHUNKS, 2)), dma((CHUNKS, 2)),
            dma((CHUNKS, 3)), dma((CHUNKS, 3)), dma((CHUNKS, 3)), dma((CHUNKS, 3)),
            dma((CHUNKS,)), dma((CHUNKS,)), dma((CHUNKS, 3)), dma((CHUNKS, 3)),
        ],
        name="window",
        compiler_params=pltpu.CompilerParams(
            collective_id=0, has_side_effects=True, vmem_limit_bytes=58 << 20
        ),
    )(tokens, cotangent, cut(gate_weight), cut(up_weight), cut(down_weight))
    return tuple(out[m].reshape(2 * SUB, d) for m in range(3))


def solution(mesh):
    in_specs = (
        P(("blk", "dp"), None),
        P(("blk", "dp"), None),
        P("blk", None),
        P("blk", None),
        P("blk", None),
    )
    out_specs = (P(("blk", "dp"), None),) * 3
    return jax.shard_map(
        functools.partial(per_device, mesh.shape["blk"]),
        mesh=mesh, in_specs=in_specs, out_specs=out_specs, check_vma=False,
    )
```
